512 devices in a mesh: tok: 64 (over y_hi, z, core), feat: 8 (over x, y_lo).
Axes of the slice: x: 4, y: 4 (y_hi: 2, y_lo: 2; y = y_hi * 2 + y_lo), z: 16, core: 2. Of those that a mesh axis runs over, the one named last changes fastest.
Arguments:
- activations: bfloat16 [32768, 16384], P('tok', 'feat'), may hold values from -300 to 300
- down_proj: bfloat16 [16384, 1024], P('feat', 'tok'), may hold values from -0.00024414062 to 0.00024414062
- precond: bfloat16 [1024, 1024], replicated, may hold values from -1 to 2, as said below
- target: bfloat16 [32768, 256], P('tok'), may hold values from -8 to 8
Outputs:
- solution: float32 [1024, 256], P('feat')
- residual: float32 [32768, 256], P('tok')
The draws below stay inside these ranges and needn't reach their ends.
Inputs may be any that keep to these rules, and one draw needn't show every extreme that they name: `precond`: upper triangular.
All inputs are finite; a program needn't handle non-finite values.
Results may differ from the reference program's by a relative error of at most 0.025.
Values may be sent and summed in bfloat16 or wider, within the bound.
No kernel may reach another device: no remote copies, remote signals or barrier semaphores. Data moves between devices by JAX's collectives and lax.ppermute only.
A program may use at most 64 MiB of HBM per device.

```python
import math
import jax
import jax.numpy as jnp
from jax import lax

H = 16384
R = 1024
K = 256
ITERS = 2
TOKENS = 32768


def draw_activations(key, part):
    key = jax.random.fold_in(key, 11)
    subkeys = jax.random.split(key, 3)
    growth = 3.0 ** (jnp.arange(TOKENS, dtype=jnp.float32) / TOKENS)
    entries = jnp.clip(jax.random.normal(subkeys[0], (TOKENS, H), jnp.float32), -5.0, 5.0)
    spread = 3.3
    row_scale = growth * jnp.exp(jax.random.uniform(subkeys[1], (TOKENS,), jnp.float32) * math.log(spread))
    col_scale = jnp.exp(jax.random.uniform(subkeys[2], (H,), jnp.float32, math.log(0.5), math.log(2.0)))
    return (entries * row_scale[:, None] * col_scale[None, :]).astype(jnp.bfloat16)


def draw_precond(key, part):
    key = jax.random.fold_in(key, 23)
    subkeys = jax.random.split(key, 2)
    diagonal = jnp.exp(jax.random.uniform(subkeys[0], (R,), jnp.float32, math.log(0.5), math.log(2.0)))
    offdiag = jnp.clip(jax.random.normal(subkeys[1], (R, R), jnp.float32), -4.0, 4.0)
    upper = jnp.triu(offdiag * (0.6 / math.sqrt(R)), 1)
    return (upper + jnp.diag(diagonal)).astype(jnp.bfloat16)


def shard_levels(key, extent, shards, smallest, largest):
    gain = 1.0
    for dim, blocks in shards:
        steps = jax.random.uniform(jax.random.fold_in(jax.random.fold_in(key, 6), dim), (blocks,), jnp.float32, smallest / len(shards), largest / len(shards))
        gain = gain * jnp.repeat(jnp.exp(steps), extent[dim] // blocks).reshape((-1,) + (1,) * (len(extent) - 1 - dim))
    return gain


def bell_draw(key, extent, width, reach, cuts=(), kind=jnp.bfloat16):
    drawn = width * jax.random.normal(key, extent, jnp.float32)
    if cuts:
        drawn = drawn * shard_levels(key, extent, cuts, -0.22, 0.18)
    return jnp.clip(drawn, -reach, reach).astype(kind)


def setup_inputs(seed: int = 0) -> dict:
    key_list = jax.random.split(jax.random.key(seed), 5)
    return {
        "activations": draw_activations(jax.random.fold_in(key_list[4], 71), 0),
        "down_proj": bell_draw(key_list[1], (H, R), (H * TOKENS) ** -0.5, 0.00024414062, ((0, 8), (1, 64))),
        "precond": draw_precond(jax.random.fold_in(key_list[4], 71), 0),
        "target": bell_draw(key_list[3], (TOKENS, K), 2.0, 8.0, ((0, 64),)),
    }


precise = lax.Precision.HIGHEST

def solve_gram(matrix, right):
    lower = jnp.linalg.cholesky(matrix)
    middle = lax.linalg.triangular_solve(lower, right, left_side=True, lower=True)
    return lax.linalg.triangular_solve(lower, middle, left_side=True, lower=True, transpose_a=True)

def reference(activations, down_proj, precond, target):
    joined = jnp.dot(activations.astype(jnp.float32), down_proj.astype(jnp.float32), preferred_element_type=jnp.float32).astype(jnp.bfloat16)

    def gradient(current):
        backed = jnp.dot(joined.T.astype(jnp.float32), current.astype(jnp.bfloat16).astype(jnp.float32), preferred_element_type=jnp.float32)
        return jnp.dot(precond.T.astype(jnp.float32), backed.astype(jnp.bfloat16).astype(jnp.float32), preferred_element_type=jnp.float32)
    residual = target.astype(jnp.float32)
    descent = gradient(residual)
    gram_now = jnp.dot(descent.T, descent, precision=precise)
    direction = descent
    solution = jnp.zeros((R, K), jnp.float32)
    for iteration in range(ITERS):
        lift = jnp.dot(precond.astype(jnp.float32), direction.astype(jnp.bfloat16).astype(jnp.float32), preferred_element_type=jnp.float32)
        image_now = jnp.dot(joined.astype(jnp.float32), lift.astype(jnp.bfloat16).astype(jnp.float32), preferred_element_type=jnp.float32)
        curvature = jnp.dot(image_now.T, image_now, precision=precise)
        step_size = solve_gram(curvature, gram_now)
        solution = solution + jnp.dot(lift, step_size, precision=precise)
        residual = residual - jnp.dot(image_now, step_size, precision=precise)
        if iteration + 1 < ITERS:
            descent = gradient(residual)
            gram_next = jnp.dot(descent.T, descent, precision=precise)
            mixing = solve_gram(gram_now, gram_next)
            direction = descent + jnp.dot(direction, mixing, precision=precise)
            gram_now = gram_next
    return (solution, residual)
```

```python
import jax
import jax.numpy as jnp
from jax import lax
from jax.experimental import pallas as pl
from jax.experimental.pallas import tpu as pltpu
from jax.sharding import Mesh, PartitionSpec as P

AXES = ("yhi", "z", "core", "x", "ylo")
TOK = ("yhi", "z", "core")
FEAT = ("x", "ylo")
BLOCK = 64
bf16 = jnp.bfloat16
f32 = jnp.float32
precise = lax.Precision.HIGHEST


def dot(a, b, ca, cb, precision=None):
    return lax.dot_general(
        a, b, (((ca,), (cb,)), ((), ())), precision=precision, preferred_element_type=f32
    )


def invert_block(d):
    n = d.shape[0]
    rows = lax.broadcasted_iota(jnp.int32, (n, n), 0)
    lanes = lax.broadcasted_iota(jnp.int32, (n, n), 1)
    lane1 = lax.broadcasted_iota(jnp.int32, (1, n), 1)
    for j in range(n):
        col = jnp.broadcast_to(d[:, j : j + 1], (n, n))
        pivot = 1.0 / col[j : j + 1, :]
        row = jnp.where(lane1 == j, pivot, d[j : j + 1, :] * pivot)
        kept = jnp.where((rows == j) | (lanes == j), 0.0, d)
        d = kept - jnp.where(rows == j, -1.0, col) * row
    return d


def invert_kernel(matrix_ref, out_ref):
    n = matrix_ref.shape[0]
    rows = lax.broadcasted_iota(jnp.int32, (n, BLOCK), 0)
    out_ref[...] = matrix_ref[...]
    for k in range(n // BLOCK):
        lo, hi = k * BLOCK, (k + 1) * BLOCK
        whole = out_ref[...]
        inverse = invert_block(whole[lo:hi, lo:hi])
        panel = dot(inverse, whole[lo:hi, :], 1, 0, precise)
        left = whole[:, lo:hi]
        inside = (rows >= lo) & (rows < hi)
        zeroed = jnp.where(inside, 0.0, left)
        update = whole - dot(zeroed, panel, 1, 0, precise)
        out_ref[...] = update
        out_ref[lo:hi, :] = panel
        out_ref[:, lo:hi] = -dot(zeroed, inverse, 1, 0, precise)
        out_ref[lo:hi, lo:hi] = inverse


def invert(matrix):
    return pl.pallas_call(
        invert_kernel,
        out_shape=jax.ShapeDtypeStruct(matrix.shape, f32),
        in_specs=[pl.BlockSpec(memory_space=pltpu.VMEM)],
        out_specs=pl.BlockSpec(memory_space=pltpu.VMEM),
        compiler_params=pltpu.CompilerParams(vmem_limit_bytes=16 * 1024 * 1024),
    )(matrix)


def swap(value, axis):
    return lax.ppermute(value, axis, [(0, 1), (1, 0)])


def shift(value, axis, by):
    n = lax.axis_size(axis)
    return lax.ppermute(value, axis, [(i, (i + by) % n) for i in range(n)])


def ordered(first, mine, other):
    return jnp.where(first, mine, other), jnp.where(first, other, mine)


def gather_columns(down_t):
    nz = lax.axis_size("z")
    z = lax.axis_index("z")
    low, high = ordered(lax.axis_index("yhi") == 0, down_t, swap(down_t, "yhi"))
    piece = jnp.stack([low, high])
    held = jnp.zeros((nz,) + piece.shape, piece.dtype)
    held = lax.dynamic_update_slice(held, piece[None], (z, 0, 0, 0))
    up = down = piece
    for k in range(1, nz // 2):
        up, down = shift(up, "z", 1), shift(down, "z", -1)
        held = lax.dynamic_update_slice(held, up[None], ((z - k) % nz, 0, 0, 0))
        held = lax.dynamic_update_slice(held, down[None], ((z + k) % nz, 0, 0, 0))
    last = jnp.stack([shift(up[0], "z", 1), shift(down[1], "z", -1)])
    return lax.dynamic_update_slice(held, last[None], ((z + nz // 2) % nz, 0, 0, 0))


def gather_by_exchange(value, axes):
    n = lax.axis_size(axes)
    spread = jnp.broadcast_to(value[None], (n,) + value.shape)
    return lax.all_to_all(spread, axes, 0, 0, tiled=True)


def halve(total, axis):
    half = total.shape[0] // 2
    here = lax.axis_index(axis)
    kept = lax.dynamic_slice_in_dim(total, here * half, half, 0)
    sent = lax.dynamic_slice_in_dim(total, (1 - here) * half, half, 0)
    return kept + swap(sent.astype(bf16), axis).astype(f32)


def on_device(activations, down_proj, precond, target):
    tokens, features = activations.shape
    rank = precond.shape[0]
    columns = target.shape[1]
    nf, nz = lax.axis_size(FEAT), lax.axis_size("z")
    feat = lax.axis_index(FEAT)
    core = lax.axis_index("core")
    share = rank // nf
    narrow = down_proj.shape[1]

    mine = gather_columns(down_proj.T).reshape(rank // 2, features)
    other = swap(mine, "core")
    map_mine = dot(activations, mine, 1, 1).astype(bf16)
    map_other = dot(activations, other, 1, 1).astype(bf16)
    partial_map = jnp.concatenate(ordered(core == 0, map_mine, map_other), axis=1)

    rows = precond.reshape(2, nz, 2, narrow, rank).transpose(2, 1, 0, 3, 4).reshape(rank, rank)

    parts = lax.all_to_all(
        partial_map.reshape(nf, tokens // nf, rank), FEAT, 0, 0, tiled=True
    )
    joined_share = jnp.sum(parts.astype(f32), axis=0).astype(bf16)
    joined = gather_by_exchange(joined_share, FEAT).reshape(tokens, rank)

    joined_slice = lax.dynamic_slice_in_dim(joined, feat * share, share, 1)
    both = jnp.concatenate([joined, target], axis=1)
    total = dot(joined_slice, both, 0, 0)
    total = halve(total, "core")
    total = halve(total, "yhi")
    quarter, width = total.shape
    parts = lax.all_to_all(
        total.astype(bf16).reshape(nz, quarter // nz, width), "z", 0, 0, tiled=True
    )
    summed = jnp.sum(parts.astype(f32), axis=0).astype(bf16)
    summed = gather_by_exchange(summed, "z").reshape(quarter, width)
    low, high = ordered(lax.axis_index("yhi") == 0, summed, swap(summed, "yhi"))
    summed = gather_by_exchange(jnp.concatenate([low, high]), FEAT)
    low, high = ordered(core == 0, summed, swap(summed, "core"))
    summed = jnp.stack([low, high], axis=1).reshape(rank, width)
    gram = summed[:, :rank]
    back = summed[:, rank:]

    own_rows = lax.dynamic_slice_in_dim(precond, feat * share, share, 0)
    descent = dot(rows, back, 0, 0)
    gram_now = dot(descent, descent, 0, 0, precise)
    direction = descent.astype(bf16)
    lift = dot(rows, direction, 1, 0)
    lift_b = lift.astype(bf16)
    image_back = dot(gram, lift_b, 1, 0)
    curvature = dot(lift_b.astype(f32), image_back, 0, 0, precise)
    inverse = invert(curvature)
    step = dot(inverse, gram_now, 1, 0, precise)
    coefficients = dot(lift, step, 1, 0, precise)
    solution = dot(dot(own_rows, direction, 1, 0), step, 1, 0, precise)

    back_next = back.astype(f32) - dot(image_back, step, 1, 0, precise)
    descent_next = dot(rows, back_next.astype(bf16), 0, 0)
    gram_next = dot(descent_next, descent_next, 0, 0, precise)
    curved = dot(rows.astype(f32), image_back, 0, 0, precise)
    mixing = -dot(inverse, dot(curved, descent_next, 0, 0, precise), 1, 0, precise)
    direction = (descent_next + dot(descent, mixing, 1, 0, precise)).astype(bf16)
    lift = dot(rows, direction, 1, 0)
    lift_b = lift.astype(bf16)
    image_back = dot(gram, lift_b, 1, 0)
    curvature = dot(lift_b.astype(f32), image_back, 0, 0, precise)
    step = dot(invert(curvature), gram_next, 1, 0, precise)
    coefficients = coefficients + dot(lift, step, 1, 0, precise)
    solution = solution + dot(dot(own_rows, direction, 1, 0), step, 1, 0, precise)
    residual = target.astype(f32) - dot(joined, coefficients.astype(bf16), 1, 0)
    return solution, residual


def solution(mesh):
    ntok, nfeat = mesh.devices.shape
    fine = Mesh(mesh.devices.reshape(2, ntok // 4, 2, nfeat // 2, 2), AXES)
    return jax.shard_map(
        on_device,
        mesh=fine,
        in_specs=(P(TOK, FEAT), P(FEAT, TOK), P(), P(TOK, None)),
        out_specs=(P(FEAT, None), P(TOK, None)),
        check_vma=False,
    )
```

```python
import jax
import jax.numpy as jnp
from jax import lax
from jax.experimental import pallas as pl
from jax.experimental.pallas import tpu as pltpu
from jax.sharding import Mesh, PartitionSpec as P

AXES = ("yhi", "z", "core", "x", "ylo")
TOK = ("yhi", "z", "core")
FEAT = ("x", "ylo")
BLOCK = 64
bf16 = jnp.bfloat16
f32 = jnp.float32
precise = lax.Precision.HIGHEST


def dot(a, b, ca, cb, precision=None):
    return lax.dot_general(
        a, b, (((ca,), (cb,)), ((), ())), precision=precision, preferred_element_type=f32
    )


def invert_block(d):
    n = d.shape[0]
    rows = lax.broadcasted_iota(jnp.int32, (n, n), 0)
    lanes = lax.broadcasted_iota(jnp.int32, (n, n), 1)
    lane1 = lax.broadcasted_iota(jnp.int32, (1, n), 1)
    for j in range(n):
        col = jnp.broadcast_to(d[:, j : j + 1], (n, n))
        pivot = 1.0 / col[j : j + 1, :]
        row = jnp.where(lane1 == j, pivot, d[j : j + 1, :] * pivot)
        kept = jnp.where((rows == j) | (lanes == j), 0.0, d)
        d = kept - jnp.where(rows == j, -1.0, col) * row
    return d


def invert_kernel(matrix_ref, out_ref):
    n = matrix_ref.shape[0]
    rows = lax.broadcasted_iota(jnp.int32, (n, BLOCK), 0)
    out_ref[...] = matrix_ref[...]
    for k in range(n // BLOCK):
        lo, hi = k * BLOCK, (k + 1) * BLOCK
        whole = out_ref[...]
        inverse = invert_block(whole[lo:hi, lo:hi])
        panel = dot(inverse, whole[lo:hi, :], 1, 0, precise)
        left = whole[:, lo:hi]
        inside = (rows >= lo) & (rows < hi)
        zeroed = jnp.where(inside, 0.0, left)
        update = whole - dot(zeroed, panel, 1, 0, precise)
        out_ref[...] = update
        out_ref[lo:hi, :] = panel
        out_ref[:, lo:hi] = -dot(zeroed, inverse, 1, 0, precise)
        out_ref[lo:hi, lo:hi] = inverse


def invert(matrix):
    return pl.pallas_call(
        invert_kernel,
        out_shape=jax.ShapeDtypeStruct(matrix.shape, f32),
        in_specs=[pl.BlockSpec(memory_space=pltpu.VMEM)],
        out_specs=pl.BlockSpec(memory_space=pltpu.VMEM),
        compiler_params=pltpu.CompilerParams(vmem_limit_bytes=16 * 1024 * 1024),
    )(matrix)


def swap(value, axis):
    return lax.ppermute(value, axis, [(0, 1), (1, 0)])


def ordered(first, mine, other):
    return jnp.where(first, mine, other), jnp.where(first, other, mine)


def gather_columns(down_t):
    nz, z_core = lax.axis_size("z"), ("z", "core")
    narrow, features = down_t.shape
    core = lax.axis_index("core")
    pair = jnp.concatenate(ordered(core == 0, down_t, swap(down_t, "core")))
    block = jnp.concatenate(ordered(lax.axis_index("yhi") == 0, pair, swap(pair, "yhi")))
    size = 4 * narrow
    ring = [(2 * z, 2 * ((z + 1) % nz)) for z in range(nz)]
    ring += [(2 * z + 1, 2 * ((z - 1) % nz) + 1) for z in range(nz)]
    held = jnp.zeros((nz * size, features), down_t.dtype)
    held = lax.dynamic_update_slice(held, block, (0, 0))
    moving = block
    for k in range(1, nz // 2):
        moving = lax.ppermute(moving, z_core, ring)
        offset = jnp.where(core == 0, nz - k, k)
        held = lax.dynamic_update_slice(held, moving, (offset * size, 0))
    half = size // 2
    far = nz // 2 * size + jnp.where(core == 0, half, 0)
    last = jnp.where(core == 0, moving[half:], moving[:half])
    held = lax.dynamic_update_slice(held, lax.ppermute(last, z_core, ring), (far, 0))
    count = nz // 2 * size - half
    here = jnp.where(core == 0, size + count, size)
    there = jnp.where(core == 0, size, size + count)
    sent = lax.dynamic_slice_in_dim(held, here, count, 0)
    return lax.dynamic_update_slice(held, swap(sent, "core"), (there, 0))


def gather_by_exchange(value, axes):
    n = lax.axis_size(axes)
    spread = jnp.broadcast_to(value[None], (n,) + value.shape)
    return lax.all_to_all(spread, axes, 0, 0, tiled=True)


def sum_by_exchange(value, axes):
    n = lax.axis_size(axes)
    parts = value.astype(bf16).reshape(n, value.shape[0] // n, value.shape[1])
    return jnp.sum(lax.all_to_all(parts, axes, 0, 0, tiled=True).astype(f32), axis=0)


def on_device(activations, down_proj, precond, target):
    tokens, features = activations.shape
    rank = precond.shape[0]
    nf, nz = lax.axis_size(FEAT), lax.axis_size("z")
    feat = lax.axis_index(FEAT)
    core = lax.axis_index("core")
    share = rank // nf
    narrow = down_proj.shape[1]

    columns_t = gather_columns(down_proj.T)
    partial_map = dot(activations, columns_t, 1, 1)

    rows = precond.reshape(2, nz, 2 * narrow, rank).transpose(1, 0, 2, 3).reshape(rank, rank)

    share_rel = sum_by_exchange(partial_map, FEAT).astype(bf16)
    start = rank - lax.axis_index("z") * (rank // nz)
    joined_share = lax.dynamic_slice_in_dim(
        jnp.concatenate([share_rel, share_rel], axis=1), start, rank, 1
    )
    joined = gather_by_exchange(joined_share, FEAT).reshape(tokens, rank)

    joined_slice = lax.dynamic_slice_in_dim(joined, feat * share, share, 1)
    total = dot(joined_slice, jnp.concatenate([joined, target], axis=1), 0, 0)
    width = total.shape[1]
    summed = sum_by_exchange(sum_by_exchange(total, ("core", "yhi")), "z").astype(bf16)
    summed = gather_by_exchange(summed, "z").reshape(share // 4, width)
    summed = gather_by_exchange(summed, ("x", "ylo", "yhi")).reshape(nf, share // 2, width)
    low, high = ordered(core == 0, summed, swap(summed, "core"))
    summed = jnp.stack([low, high], axis=1).reshape(rank, width)
    gram = summed[:, :rank]
    back = summed[:, rank:]

    own_rows = lax.dynamic_slice_in_dim(precond, feat * share, share, 0)
    descent = dot(rows, back, 0, 0)
    gram_now = dot(descent, descent, 0, 0, precise)
    direction = descent.astype(bf16)
    lift = dot(rows, direction, 1, 0)
    lift_b = lift.astype(bf16)
    image_back = dot(gram, lift_b, 1, 0)
    curvature = dot(lift_b.astype(f32), image_back, 0, 0, precise)
    inverse = invert(curvature)
    step = dot(inverse, gram_now, 1, 0, precise)
    coefficients = dot(lift, step, 1, 0, precise)
    solution = dot(dot(own_rows, direction, 1, 0), step, 1, 0, precise)

    back_next = back.astype(f32) - dot(image_back, step, 1, 0, precise)
    descent_next = dot(rows, back_next.astype(bf16), 0, 0)
    gram_next = dot(descent_next, descent_next, 0, 0, precise)
    curved = dot(rows.astype(f32), image_back, 0, 0, precise)
    mixing = -dot(inverse, dot(curved, descent_next, 0, 0, precise), 1, 0, precise)
    direction = (descent_next + dot(descent, mixing, 1, 0, precise)).astype(bf16)
    lift = dot(rows, direction, 1, 0)
    lift_b = lift.astype(bf16)
    image_back = dot(gram, lift_b, 1, 0)
    curvature = dot(lift_b.astype(f32), image_back, 0, 0, precise)
    step = dot(invert(curvature), gram_next, 1, 0, precise)
    coefficients = coefficients + dot(lift, step, 1, 0, precise)
    solution = solution + dot(dot(own_rows, direction, 1, 0), step, 1, 0, precise)
    residual = target.astype(f32) - dot(joined, coefficients.astype(bf16), 1, 0)
    return solution, residual


def solution(mesh):
    ntok, nfeat = mesh.devices.shape
    fine = Mesh(mesh.devices.reshape(2, ntok // 4, 2, nfeat // 2, 2), AXES)
    return jax.shard_map(
        on_device,
        mesh=fine,
        in_specs=(P(TOK, FEAT), P(FEAT, TOK), P(), P(TOK, None)),
        out_specs=(P(FEAT, None), P(TOK, None)),
        check_vma=False,
    )
```

```python
import jax
import jax.numpy as jnp
from jax import lax
from jax.experimental import pallas as pl
from jax.experimental.pallas import tpu as pltpu
from jax.sharding import Mesh, PartitionSpec as P

AXES = ("yhi", "z", "core", "x", "ylo")
TOK = ("yhi", "z", "core")
FEAT = ("x", "ylo")
BLOCK = 128
bf16 = jnp.bfloat16
f32 = jnp.float32
precise = lax.Precision.HIGHEST
three = lax.Precision.HIGH


def dot(a, b, ca, cb, precision=None):
    return lax.dot_general(
        a, b, (((ca,), (cb,)), ((), ())), precision=precision, preferred_element_type=f32
    )


def invert_block(d):
    n = d.shape[0]
    lanes = lax.broadcasted_iota(jnp.int32, (8, n), 1)
    subs = lax.broadcasted_iota(jnp.int32, (8, n), 0)

    def lane(v, j):
        return jnp.broadcast_to(v[:, j : j + 1], (8, n))

    def row(v, j):
        return jnp.broadcast_to(v[j : j + 1, :], (8, n))

    tiles = [d[i : i + 8, :] for i in range(0, n, 8)]
    count = len(tiles)
    for p in range(count):
        lo = 8 * p
        pivots = [lane(tiles[p], lo + k) for k in range(8)]
        for j in range(8):
            at = subs == j
            scale = 1.0 / row(pivots[j], j)
            minus = -pivots[j]
            fresh = []
            for k in range(8):
                if k == j:
                    fresh.append(jnp.where(at, scale, minus * scale))
                else:
                    scaled = row(pivots[k], j) * scale
                    fresh.append(jnp.where(at, scaled, pivots[k] + minus * scaled))
            pivots = fresh
        inside = (lanes >= lo) & (lanes < lo + 8)
        panel = jnp.where(inside, jnp.where(lanes - lo == subs, 1.0, 0.0), tiles[p])
        scaled = pivots[0] * row(panel, 0)
        for k in range(1, 8):
            scaled = scaled + pivots[k] * row(panel, k)
        rows = [row(scaled, k) for k in range(8)]
        for i in [(p + 1 + i) % count for i in range(count - 1)]:
            even = lane(tiles[i], lo) * rows[0]
            odd = lane(tiles[i], lo + 1) * rows[1]
            for k in range(2, 8, 2):
                even = even + lane(tiles[i], lo + k) * rows[k]
                odd = odd + lane(tiles[i], lo + k + 1) * rows[k + 1]
            tiles[i] = jnp.where(inside, 0.0, tiles[i]) - (even + odd)
        tiles[p] = scaled
    return jnp.concatenate(tiles, axis=0)


def invert_kernel(matrix_ref, out_ref):
    n = matrix_ref.shape[0]
    rows = lax.broadcasted_iota(jnp.int32, (n, BLOCK), 0)
    out_ref[...] = matrix_ref[...]
    for k in range(n // BLOCK):
        lo, hi = k * BLOCK, (k + 1) * BLOCK
        inverse = invert_block(out_ref[lo:hi, lo:hi])
        left = out_ref[:, lo:hi]
        zeroed = jnp.where((rows >= lo) & (rows < hi), 0.0, left)
        out_ref[lo:hi, :] = dot(inverse, out_ref[lo:hi, :], 1, 0, precise)
        out_ref[lo:hi, lo:hi] = inverse
        panel = out_ref[lo:hi, :]
        out_ref[lo:hi, :] = jnp.zeros_like(panel)
        out_ref[:, lo:hi] = jnp.zeros_like(left)
        out_ref[...] = out_ref[...] - dot(zeroed, panel, 1, 0, precise)
        out_ref[lo:hi, :] = panel


def invert(matrix):
    return pl.pallas_call(
        invert_kernel,
        out_shape=jax.ShapeDtypeStruct(matrix.shape, f32),
        in_specs=[pl.BlockSpec(memory_space=pltpu.VMEM)],
        out_specs=pl.BlockSpec(memory_space=pltpu.VMEM),
        compiler_params=pltpu.CompilerParams(vmem_limit_bytes=16 * 1024 * 1024),
    )(matrix)


def swap(value, axis):
    return lax.ppermute(value, axis, [(0, 1), (1, 0)])


def ordered(first, mine, other):
    return jnp.where(first, mine, other), jnp.where(first, other, mine)


def shift(value, axis, by):
    n = lax.axis_size(axis)
    return lax.ppermute(value, axis, [(i, (i + by) % n) for i in range(n)])


def gather_columns(down_t):
    low, high = ordered(lax.axis_index("yhi") == 0, down_t, swap(down_t, "yhi"))
    block = jnp.concatenate([low, high])
    narrow = down_t.shape[0]
    up, down = block, block
    below, above = [], []
    for k in range(1, lax.axis_size("z") // 2):
        up, down = shift(up, "z", 1), shift(down, "z", -1)
        below.append(up)
        above.append(down)
    last = [shift(up[:narrow], "z", 1), shift(down[narrow:], "z", -1)]
    return jnp.concatenate([block] + above + last + below[::-1])


def gather_by_exchange(value, axes):
    n = lax.axis_size(axes)
    spread = jnp.broadcast_to(value[None], (n,) + value.shape)
    return lax.all_to_all(spread, axes, 0, 0, tiled=True)


def sum_by_exchange(value, axes):
    n = lax.axis_size(axes)
    parts = value.astype(bf16).reshape(n, value.shape[0] // n, value.shape[1])
    return jnp.sum(lax.all_to_all(parts, axes, 0, 0, tiled=True).astype(f32), axis=0)


def on_device(activations, down_proj, precond, target):
    tokens, features = activations.shape
    rank = precond.shape[0]
    nf, nz = lax.axis_size(FEAT), lax.axis_size("z")
    feat = lax.axis_index(FEAT)
    core = lax.axis_index("core")
    share = rank // nf
    narrow = down_proj.shape[1]

    mine = gather_columns(down_proj.T)
    other = swap(mine, "core")
    map_mine = dot(activations, mine, 1, 1).astype(bf16)
    map_other = dot(activations, other, 1, 1).astype(bf16)
    partial_map = jnp.concatenate(ordered(core == 0, map_mine, map_other), axis=1)

    rows = precond.reshape(2, nz, 2, narrow, rank).transpose(2, 1, 0, 3, 4).reshape(rank, rank)

    share_rel = sum_by_exchange(partial_map, FEAT).astype(bf16)
    half = rank // 2
    start = half - lax.axis_index("z") * (half // nz)
    joined_share = jnp.concatenate(
        [
            lax.dynamic_slice_in_dim(jnp.concatenate([part, part], axis=1), start, half, 1)
            for part in (share_rel[:, :half], share_rel[:, half:])
        ],
        axis=1,
    )
    joined = gather_by_exchange(joined_share, FEAT).reshape(tokens, rank)

    joined_slice = lax.dynamic_slice_in_dim(joined, feat * share, share, 1)
    total = dot(joined_slice, jnp.concatenate([joined, target], axis=1), 0, 0)
    width = total.shape[1]
    summed = sum_by_exchange(sum_by_exchange(total, ("core", "yhi")), "z").astype(bf16)
    summed = gather_by_exchange(summed, "z").reshape(share // 4, width)
    summed = gather_by_exchange(summed, ("x", "ylo", "yhi")).reshape(nf, share // 2, width)
    low, high = ordered(core == 0, summed, swap(summed, "core"))
    summed = jnp.stack([low, high], axis=1).reshape(rank, width)
    gram = summed[:, :rank]
    back = summed[:, rank:]

    descent = dot(rows, back, 0, 0)
    gram_now = dot(descent, descent, 0, 0, three)
    lift = dot(rows, descent.astype(bf16), 1, 0)
    lift_b = lift.astype(bf16)
    image_back = dot(gram, lift_b, 1, 0)
    curvature = dot(lift_b.astype(f32), image_back, 0, 0, three)
    inverse = invert(curvature)
    step = dot(inverse, gram_now, 1, 0, three)

    coarse = image_back.astype(bf16)
    fine = (image_back - coarse.astype(f32)).astype(bf16)
    curved = dot(rows, coarse, 0, 0) + dot(rows, fine, 0, 0)
    descent_next = descent - dot(curved, step, 1, 0, three)
    gram_next = dot(descent_next, descent_next, 0, 0, three)
    mixing = dot(inverse, dot(curved, descent_next, 0, 0, three), 1, 0, three)
    direction = descent_next - dot(descent, mixing, 1, 0, three)
    lift_next = dot(rows, direction.astype(bf16), 1, 0)
    lift_b = lift_next.astype(bf16)
    curvature = dot(lift_b.astype(f32), dot(gram, lift_b, 1, 0), 0, 0, three)
    step_next = dot(invert(curvature), gram_next, 1, 0, three)

    coefficients = dot(lift, step, 1, 0, three) + dot(lift_next, step_next, 1, 0, three)
    residual = target.astype(f32) - dot(joined, coefficients.astype(bf16), 1, 0)
    part = nz * 2 // nf
    kept = coefficients.reshape(2, nz, 2, narrow, -1).transpose(2, 1, 0, 3, 4)
    kept = kept.reshape(nf, part, 2, narrow, -1)
    solution = lax.dynamic_index_in_dim(kept, feat, 0, keepdims=False).reshape(share, -1)
    return solution, residual


def solution(mesh):
    ntok, nfeat = mesh.devices.shape
    fine = Mesh(mesh.devices.reshape(2, ntok // 4, 2, nfeat // 2, 2), AXES)
    return jax.shard_map(
        on_device,
        mesh=fine,
        in_specs=(P(TOK, FEAT), P(FEAT, TOK), P(), P(TOK, None)),
        out_specs=(P(FEAT, None), P(TOK, None)),
        check_vma=False,
    )
```

```python
import jax
import jax.numpy as jnp
from jax import lax
from jax.experimental import pallas as pl
from jax.experimental.pallas import tpu as pltpu
from jax.sharding import Mesh, PartitionSpec as P

AXES = ("yhi", "z", "core", "x", "ylo")
TOK = ("yhi", "z", "core")
FEAT = ("x", "ylo")
BLOCK = 128
bf16 = jnp.bfloat16
f32 = jnp.float32
precise = lax.Precision.HIGHEST
three = lax.Precision.HIGH


def dot(a, b, ca, cb, precision=None):
    return lax.dot_general(
        a, b, (((ca,), (cb,)), ((), ())), precision=precision, preferred_element_type=f32
    )


def invert_block(d):
    n = d.shape[0]
    lanes = lax.broadcasted_iota(jnp.int32, (8, n), 1)
    subs = lax.broadcasted_iota(jnp.int32, (8, n), 0)

    def lane(v, j):
        return jnp.broadcast_to(v[:, j : j + 1], (8, n))

    def row(v, j):
        return jnp.broadcast_to(v[j : j + 1, :], (8, n))

    tiles = [d[i : i + 8, :] for i in range(0, n, 8)]
    count = len(tiles)
    for p in range(count):
        lo = 8 * p
        pivots = [lane(tiles[p], lo + k) for k in range(8)]
        for j in range(8):
            at = subs == j
            scale = 1.0 / row(pivots[j], j)
            minus = -pivots[j]
            fresh = []
            for k in range(8):
                if k == j:
                    fresh.append(jnp.where(at, scale, minus * scale))
                else:
                    scaled = row(pivots[k], j) * scale
                    fresh.append(jnp.where(at, scaled, pivots[k] + minus * scaled))
            pivots = fresh
        inside = (lanes >= lo) & (lanes < lo + 8)
        panel = jnp.where(inside, jnp.where(lanes - lo == subs, 1.0, 0.0), tiles[p])
        scaled = pivots[0] * row(panel, 0)
        for k in range(1, 8):
            scaled = scaled + pivots[k] * row(panel, k)
        rows = [row(scaled, k) for k in range(8)]
        for i in [(p + 1 + i) % count for i in range(count - 1)]:
            even = lane(tiles[i], lo) * rows[0]
            odd = lane(tiles[i], lo + 1) * rows[1]
            for k in range(2, 8, 2):
                even = even + lane(tiles[i], lo + k) * rows[k]
                odd = odd + lane(tiles[i], lo + k + 1) * rows[k + 1]
            tiles[i] = jnp.where(inside, 0.0, tiles[i]) - (even + odd)
        tiles[p] = scaled
    return jnp.concatenate(tiles, axis=0)


def invert_kernel(matrix_ref, out_ref):
    n = matrix_ref.shape[0]
    rows = lax.broadcasted_iota(jnp.int32, (n, BLOCK), 0)
    out_ref[...] = matrix_ref[...]
    for k in range(n // BLOCK):
        lo, hi = k * BLOCK, (k + 1) * BLOCK
        inverse = invert_block(out_ref[lo:hi, lo:hi])
        left = out_ref[:, lo:hi]
        zeroed = jnp.where((rows >= lo) & (rows < hi), 0.0, left)
        out_ref[lo:hi, :] = dot(inverse, out_ref[lo:hi, :], 1, 0, precise)
        out_ref[lo:hi, lo:hi] = inverse
        panel = out_ref[lo:hi, :]
        out_ref[lo:hi, :] = jnp.zeros_like(panel)
        out_ref[:, lo:hi] = jnp.zeros_like(left)
        out_ref[...] = out_ref[...] - dot(zeroed, panel, 1, 0, precise)
        out_ref[lo:hi, :] = panel


def invert(matrix):
    return pl.pallas_call(
        invert_kernel,
        out_shape=jax.ShapeDtypeStruct(matrix.shape, f32),
        in_specs=[pl.BlockSpec(memory_space=pltpu.VMEM)],
        out_specs=pl.BlockSpec(memory_space=pltpu.VMEM),
        compiler_params=pltpu.CompilerParams(vmem_limit_bytes=16 * 1024 * 1024),
    )(matrix)


def swap(value, axis):
    return lax.ppermute(value, axis, [(0, 1), (1, 0)])


def ordered(first, mine, other):
    return jnp.where(first, mine, other), jnp.where(first, other, mine)


def shift(value, axis, by):
    n = lax.axis_size(axis)
    return lax.ppermute(value, axis, [(i, (i + by) % n) for i in range(n)])


def gather_columns(down_t):
    half = down_t.shape[0] // 2
    up, down = down_t, down_t
    below, above = [], []
    for k in range(1, lax.axis_size("z") // 2):
        up, down = shift(up, "z", 1), shift(down, "z", -1)
        below.append(up)
        above.append(down)
    last = [shift(up[:half], "z", 1), shift(down[half:], "z", -1)]
    return jnp.concatenate([down_t] + above + last + below[::-1])


def gather_by_exchange(value, axes):
    n = lax.axis_size(axes)
    spread = jnp.broadcast_to(value[None], (n,) + value.shape)
    return lax.all_to_all(spread, axes, 0, 0, tiled=True)


def sum_by_exchange(value, axes):
    n = lax.axis_size(axes)
    parts = value.astype(bf16).reshape(n, value.shape[0] // n, value.shape[1])
    return jnp.sum(lax.all_to_all(parts, axes, 0, 0, tiled=True).astype(f32), axis=0)


def on_device(activations, down_proj, precond, target):
    tokens, features = activations.shape
    rank = precond.shape[0]
    nf, nz = lax.axis_size(FEAT), lax.axis_size("z")
    feat = lax.axis_index(FEAT)
    core = lax.axis_index("core")
    share = rank // nf
    narrow = down_proj.shape[1]

    partner = swap(activations, "yhi")
    mine = gather_columns(down_proj.T)
    columns_t = jnp.concatenate([mine, swap(mine, "core")])
    partial_map = jnp.stack(
        [
            dot(part, columns_t, 1, 1).astype(bf16).reshape(nf, tokens // nf, rank // 2)
            for part in (activations, partner)
        ],
        axis=1,
    )
    share_rel = sum_by_exchange(partial_map.reshape(2 * tokens, rank // 2), FEAT).astype(bf16)

    quarter = rank // 4
    start = quarter - lax.axis_index("z") * narrow
    turned = [
        lax.dynamic_slice_in_dim(jnp.concatenate([part, part], axis=1), start, quarter, 1)
        for part in (share_rel[:, :quarter], share_rel[:, quarter:])
    ]
    turned = jnp.concatenate(ordered(core == 0, *turned), axis=1)
    own, other = turned[: tokens // nf], turned[tokens // nf :]
    spread = jnp.stack(ordered(lax.axis_index("yhi") == 0, own, other))
    spread = jnp.broadcast_to(spread[None], (nf,) + spread.shape)
    plane = ("x", "ylo", "yhi")
    halves = lax.all_to_all(
        spread.reshape(2 * nf, tokens // nf, rank // 2), plane, 0, 0, tiled=True
    ).reshape(nf, 2, tokens // nf, rank // 2)
    joined = jnp.concatenate([halves[:, 0], halves[:, 1]], axis=2).reshape(tokens, rank)

    rows = precond.reshape(2, nz, 2, narrow, rank).transpose(0, 2, 1, 3, 4).reshape(rank, rank)

    joined_slice = lax.dynamic_slice_in_dim(joined, feat * share, share, 1)
    total = dot(joined_slice, jnp.concatenate([joined, target], axis=1), 0, 0)
    width = total.shape[1]
    summed = sum_by_exchange(sum_by_exchange(total, ("core", "yhi")), "z").astype(bf16)
    summed = gather_by_exchange(summed, "z").reshape(share // 4, width)
    summed = gather_by_exchange(summed, plane).reshape(nf, share // 2, width)
    low, high = ordered(core == 0, summed, swap(summed, "core"))
    summed = jnp.stack([low, high], axis=1).reshape(rank, width)
    gram = summed[:, :rank]
    back = summed[:, rank:]

    descent = dot(rows, back, 0, 0)
    gram_now = dot(descent, descent, 0, 0, three)
    lift = dot(rows, descent.astype(bf16), 1, 0)
    lift_b = lift.astype(bf16)
    image_back = dot(gram, lift_b, 1, 0)
    curvature = dot(lift_b.astype(f32), image_back, 0, 0, three)
    inverse = invert(curvature)
    step = dot(inverse, gram_now, 1, 0, three)

    coarse = image_back.astype(bf16)
    fine = (image_back - coarse.astype(f32)).astype(bf16)
    curved = dot(rows, coarse, 0, 0) + dot(rows, fine, 0, 0)
    descent_next = descent - dot(curved, step, 1, 0, three)
    gram_next = dot(descent_next, descent_next, 0, 0, three)
    mixing = dot(inverse, dot(curved, descent_next, 0, 0, three), 1, 0, three)
    direction = descent_next - dot(descent, mixing, 1, 0, three)
    lift_next = dot(rows, direction.astype(bf16), 1, 0)
    lift_b = lift_next.astype(bf16)
    curvature = dot(lift_b.astype(f32), dot(gram, lift_b, 1, 0), 0, 0, three)
    step_next = dot(invert(curvature), gram_next, 1, 0, three)

    coefficients = dot(lift, step, 1, 0, three) + dot(lift_next, step_next, 1, 0, three)
    residual = target.astype(f32) - dot(joined, coefficients.astype(bf16), 1, 0)
    part = nz * 2 // nf
    kept = coefficients.reshape(2, 2, nz, narrow, -1).transpose(0, 2, 1, 3, 4)
    kept = kept.reshape(nf, part, 2, narrow, -1)
    solution = lax.dynamic_index_in_dim(kept, feat, 0, keepdims=False).reshape(share, -1)
    return solution, residual


def solution(mesh):
    ntok, nfeat = mesh.devices.shape
    fine = Mesh(mesh.devices.reshape(2, ntok // 4, 2, nfeat // 2, 2), AXES)
    return jax.shard_map(
        on_device,
        mesh=fine,
        in_specs=(P(TOK, FEAT), P(FEAT, TOK), P(), P(TOK, None)),
        out_specs=(P(FEAT, None), P(TOK, None)),
        check_vma=False,
    )
```

```python
import jax
import jax.numpy as jnp
from jax import lax
from jax.experimental import pallas as pl
from jax.experimental.pallas import tpu as pltpu
from jax.sharding import Mesh, PartitionSpec as P

AXES = ("yhi", "z", "core", "x", "ylo")
TOK = ("yhi", "z", "core")
FEAT = ("x", "ylo")
bf16 = jnp.bfloat16
f32 = jnp.float32
precise = lax.Precision.HIGHEST
three = lax.Precision.HIGH


def dot(a, b, ca, cb, precision=None):
    return lax.dot_general(
        a, b, (((ca,), (cb,)), ((), ())), precision=precision, preferred_element_type=f32
    )


def invert_block(d):
    n = d.shape[0]
    lanes = lax.broadcasted_iota(jnp.int32, (8, n), 1)
    subs = lax.broadcasted_iota(jnp.int32, (8, n), 0)

    def lane(v, j):
        return jnp.broadcast_to(v[:, j : j + 1], (8, n))

    def row(v, j):
        return jnp.broadcast_to(v[j : j + 1, :], (8, n))

    tiles = [d[i : i + 8, :] for i in range(0, n, 8)]
    count = len(tiles)
    for p in range(count):
        lo = 8 * p
        pivots = [lane(tiles[p], lo + k) for k in range(8)]
        for j in range(8):
            at = subs == j
            scale = 1.0 / row(pivots[j], j)
            minus = -pivots[j]
            fresh = []
            for k in range(8):
                if k == j:
                    fresh.append(jnp.where(at, scale, minus * scale))
                else:
                    scaled = row(pivots[k], j) * scale
                    fresh.append(jnp.where(at, scaled, pivots[k] + minus * scaled))
            pivots = fresh
        inside = (lanes >= lo) & (lanes < lo + 8)
        panel = jnp.where(inside, jnp.where(lanes - lo == subs, 1.0, 0.0), tiles[p])
        scaled = pivots[0] * row(panel, 0)
        for k in range(1, 8):
            scaled = scaled + pivots[k] * row(panel, k)
        rows = [row(scaled, k) for k in range(8)]
        for i in [(p + 1 + i) % count for i in range(count - 1)]:
            even = lane(tiles[i], lo) * rows[0]
            odd = lane(tiles[i], lo + 1) * rows[1]
            for k in range(2, 8, 2):
                even = even + lane(tiles[i], lo + k) * rows[k]
                odd = odd + lane(tiles[i], lo + k + 1) * rows[k + 1]
            tiles[i] = jnp.where(inside, 0.0, tiles[i]) - (even + odd)
        tiles[p] = scaled
    return jnp.concatenate(tiles, axis=0)


def invert_kernel(matrix_ref, out_ref):
    half = matrix_ref.shape[0] // 2
    first = invert_block(matrix_ref[:half, :half])
    corner = matrix_ref[:half, half:]
    right = dot(first, corner, 1, 0, precise)
    last = invert_block(matrix_ref[half:, half:] - dot(corner, right, 0, 0, precise))
    cross = dot(right, last, 1, 0, precise)
    out_ref[:half, :half] = first + dot(cross, right, 1, 1, precise)
    out_ref[:half, half:] = -cross
    out_ref[half:, :half] = -cross.T
    out_ref[half:, half:] = last


def invert(matrix):
    return pl.pallas_call(
        invert_kernel,
        out_shape=jax.ShapeDtypeStruct(matrix.shape, f32),
        in_specs=[pl.BlockSpec(memory_space=pltpu.VMEM)],
        out_specs=pl.BlockSpec(memory_space=pltpu.VMEM),
        compiler_params=pltpu.CompilerParams(vmem_limit_bytes=16 * 1024 * 1024),
    )(matrix)


def swap(value, axis):
    return lax.ppermute(value, axis, [(0, 1), (1, 0)])


def ordered(first, mine, other):
    return jnp.where(first, mine, other), jnp.where(first, other, mine)


def shift(value, axis, by):
    n = lax.axis_size(axis)
    return lax.ppermute(value, axis, [(i, (i + by) % n) for i in range(n)])


def gather_columns(down_t):
    n = down_t.shape[0]
    half = n // 2
    nz = lax.axis_size("z")
    if nz != 16:
        up, down = down_t, down_t
        below, above = [], []
        for k in range(1, nz // 2):
            up, down = shift(up, "z", 1), shift(down, "z", -1)
            below.append(up)
            above.append(down)
        last = [shift(up[:half], "z", 1), shift(down[half:], "z", -1)]
        return jnp.concatenate([down_t] + above + last + below[::-1])
    below_1, above_1 = shift(down_t, "z", 1), shift(down_t, "z", -1)
    below_2 = shift(jnp.concatenate([down_t, below_1]), "z", 2)
    above_2 = shift(jnp.concatenate([down_t, above_1]), "z", -2)
    below_4, above_4 = shift(below_2, "z", 2), shift(above_2, "z", -2)
    below_6 = shift(jnp.concatenate([below_2[n:], below_4[: n + half]]), "z", 3)
    above_6 = shift(
        jnp.concatenate([above_2[n:], above_4[:n], above_4[n + half :]]), "z", -3
    )
    above = [down_t, above_1, above_2, above_4, above_6[: 2 * n]]
    far = [below_6[2 * n :], above_6[2 * n :]]
    below = []
    for pair in (below_6, below_4, below_2):
        below += [pair[n : 2 * n], pair[:n]]
    return jnp.concatenate(above + far + below + [below_1])


def gather_by_exchange(value, axes):
    n = lax.axis_size(axes)
    spread = jnp.broadcast_to(value[None], (n,) + value.shape)
    return lax.all_to_all(spread, axes, 0, 0, tiled=True)


def sum_by_exchange(value, axes):
    n = lax.axis_size(axes)
    parts = value.astype(bf16).reshape(n, value.shape[0] // n, value.shape[1])
    return jnp.sum(lax.all_to_all(parts, axes, 0, 0, tiled=True).astype(f32), axis=0)


def on_device(activations, down_proj, precond, target):
    tokens, features = activations.shape
    rank = precond.shape[0]
    nf, nz = lax.axis_size(FEAT), lax.axis_size("z")
    feat = lax.axis_index(FEAT)
    core = lax.axis_index("core")
    share = rank // nf
    narrow = down_proj.shape[1]

    partner = swap(activations, "yhi")
    mine = gather_columns(down_proj.T)
    columns_t = jnp.concatenate([mine, swap(mine, "core")])
    partial_map = jnp.stack(
        [
            dot(part, columns_t, 1, 1).astype(bf16).reshape(nf, tokens // nf, rank // 2)
            for part in (activations, partner)
        ],
        axis=1,
    )
    share_rel = sum_by_exchange(partial_map.reshape(2 * tokens, rank // 2), FEAT).astype(bf16)

    quarter = rank // 4
    start = quarter - lax.axis_index("z") * narrow
    turned = [
        lax.dynamic_slice_in_dim(jnp.concatenate([part, part], axis=1), start, quarter, 1)
        for part in (share_rel[:, :quarter], share_rel[:, quarter:])
    ]
    turned = jnp.concatenate(ordered(core == 0, *turned), axis=1)
    own, other = turned[: tokens // nf], turned[tokens // nf :]
    spread = jnp.stack(ordered(lax.axis_index("yhi") == 0, own, other))
    spread = jnp.broadcast_to(spread[None], (nf,) + spread.shape)
    plane = ("x", "ylo", "yhi")
    halves = lax.all_to_all(
        spread.reshape(2 * nf, tokens // nf, rank // 2), plane, 0, 0, tiled=True
    ).reshape(nf, 2, tokens // nf, rank // 2)
    joined = jnp.concatenate([halves[:, 0], halves[:, 1]], axis=2).reshape(tokens, rank)

    rows = precond.reshape(2, nz, 2, narrow, rank).transpose(0, 2, 1, 3, 4).reshape(rank, rank)

    joined_slice = lax.dynamic_slice_in_dim(joined, feat * share, share, 1)
    total = dot(joined_slice, jnp.concatenate([joined, target], axis=1), 0, 0)
    width = total.shape[1]
    summed = sum_by_exchange(sum_by_exchange(total, ("core", "yhi")), "z").astype(bf16)
    summed = gather_by_exchange(summed, "z").reshape(share // 4, width)
    summed = gather_by_exchange(summed, plane).reshape(nf, share // 2, width)
    low, high = ordered(core == 0, summed, swap(summed, "core"))
    summed = jnp.stack([low, high], axis=1).reshape(rank, width)
    gram = summed[:, :rank]
    back = summed[:, rank:]

    descent = dot(rows, back, 0, 0)
    gram_now = dot(descent, descent, 0, 0, three)
    lift = dot(rows, descent.astype(bf16), 1, 0)
    lift_b = lift.astype(bf16)
    image_back = dot(gram, lift_b, 1, 0)
    curvature = dot(lift_b.astype(f32), image_back, 0, 0, three)
    inverse = invert(curvature)
    step = dot(inverse, gram_now, 1, 0, three)

    coarse = image_back.astype(bf16)
    fine = (image_back - coarse.astype(f32)).astype(bf16)
    curved = dot(rows, coarse, 0, 0) + dot(rows, fine, 0, 0)
    descent_next = descent - dot(curved, step, 1, 0, three)
    gram_next = dot(descent_next, descent_next, 0, 0, three)
    mixing = dot(inverse, dot(curved, descent_next, 0, 0, three), 1, 0, three)
    direction = descent_next - dot(descent, mixing, 1, 0, three)
    lift_next = dot(rows, direction.astype(bf16), 1, 0)
    lift_b = lift_next.astype(bf16)
    curvature = dot(lift_b.astype(f32), dot(gram, lift_b, 1, 0), 0, 0, three)
    step_next = dot(invert(curvature), gram_next, 1, 0, three)

    coefficients = dot(lift, step, 1, 0, three) + dot(lift_next, step_next, 1, 0, three)
    residual = target.astype(f32) - dot(joined, coefficients.astype(bf16), 1, 0)
    part = nz * 2 // nf
    kept = coefficients.reshape(2, 2, nz, narrow, -1).transpose(0, 2, 1, 3, 4)
    kept = kept.reshape(nf, part, 2, narrow, -1)
    solution = lax.dynamic_index_in_dim(kept, feat, 0, keepdims=False).reshape(share, -1)
    return solution, residual


def solution(mesh):
    ntok, nfeat = mesh.devices.shape
    fine = Mesh(mesh.devices.reshape(2, ntok // 4, 2, nfeat // 2, 2), AXES)
    return jax.shard_map(
        on_device,
        mesh=fine,
        in_specs=(P(TOK, FEAT), P(FEAT, TOK), P(), P(TOK, None)),
        out_specs=(P(FEAT, None), P(TOK, None)),
        check_vma=False,
    )
```

```python
import jax
import jax.numpy as jnp
from jax import lax
from jax.experimental import pallas as pl
from jax.experimental.pallas import tpu as pltpu
from jax.sharding import Mesh, PartitionSpec as P

AXES = ("yhi", "z", "core", "x", "ylo")
TOK = ("yhi", "z", "core")
FEAT = ("x", "ylo")
bf16 = jnp.bfloat16
f32 = jnp.float32
precise = lax.Precision.HIGHEST
three = lax.Precision.HIGH


def dot(a, b, ca, cb, precision=None):
    return lax.dot_general(
        a, b, (((ca,), (cb,)), ((), ())), precision=precision, preferred_element_type=f32
    )


def invert_block(d):
    n = d.shape[0]
    lanes = lax.broadcasted_iota(jnp.int32, (8, n), 1)
    subs = lax.broadcasted_iota(jnp.int32, (8, n), 0)

    def lane(v, j):
        return jnp.broadcast_to(v[:, j : j + 1], (8, n))

    def row(v, j):
        return jnp.broadcast_to(v[j : j + 1, :], (8, n))

    tiles = [d[i : i + 8, :] for i in range(0, n, 8)]
    count = len(tiles)
    for p in range(count):
        lo = 8 * p
        pivots = [lane(tiles[p], lo + k) for k in range(8)]
        for j in range(8):
            at = subs == j
            scale = 1.0 / row(pivots[j], j)
            minus = -pivots[j]
            fresh = []
            for k in range(8):
                if k == j:
                    fresh.append(jnp.where(at, scale, minus * scale))
                else:
                    scaled = row(pivots[k], j) * scale
                    fresh.append(jnp.where(at, scaled, pivots[k] + minus * scaled))
            pivots = fresh
        inside = (lanes >= lo) & (lanes < lo + 8)
        panel = jnp.where(inside, jnp.where(lanes - lo == subs, 1.0, 0.0), tiles[p])
        scaled = pivots[0] * row(panel, 0)
        for k in range(1, 8):
            scaled = scaled + pivots[k] * row(panel, k)
        rows = [row(scaled, k) for k in range(8)]
        for i in [(p + 1 + i) % count for i in range(count - 1)]:
            even = lane(tiles[i], lo) * rows[0]
            odd = lane(tiles[i], lo + 1) * rows[1]
            for k in range(2, 8, 2):
                even = even + lane(tiles[i], lo + k) * rows[k]
                odd = odd + lane(tiles[i], lo + k + 1) * rows[k + 1]
            tiles[i] = jnp.where(inside, 0.0, tiles[i]) - (even + odd)
        tiles[p] = scaled
    return jnp.concatenate(tiles, axis=0)


def invert_kernel(matrix_ref, out_ref):
    half = matrix_ref.shape[0] // 2
    first = invert_block(matrix_ref[:half, :half])
    corner = matrix_ref[:half, half:]
    right = dot(first, corner, 1, 0, precise)
    last = invert_block(matrix_ref[half:, half:] - dot(corner, right, 0, 0, precise))
    cross = dot(right, last, 1, 0, precise)
    out_ref[:half, :half] = first + dot(cross, right, 1, 1, precise)
    out_ref[:half, half:] = -cross
    out_ref[half:, :half] = -cross.T
    out_ref[half:, half:] = last


def invert(matrix):
    return pl.pallas_call(
        invert_kernel,
        out_shape=jax.ShapeDtypeStruct(matrix.shape, f32),
        in_specs=[pl.BlockSpec(memory_space=pltpu.VMEM)],
        out_specs=pl.BlockSpec(memory_space=pltpu.VMEM),
        compiler_params=pltpu.CompilerParams(vmem_limit_bytes=16 * 1024 * 1024),
    )(matrix)


def swap(value, axis):
    return lax.ppermute(value, axis, [(0, 1), (1, 0)])


def ordered(first, mine, other):
    return jnp.where(first, mine, other), jnp.where(first, other, mine)


def shift(value, axis, by):
    n = lax.axis_size(axis)
    return lax.ppermute(value, axis, [(i, (i + by) % n) for i in range(n)])


def gather_columns(down_t):
    n = down_t.shape[0]
    half = n // 2
    nz = lax.axis_size("z")
    if nz != 16:
        up, down = down_t, down_t
        below, above = [], []
        for k in range(1, nz // 2):
            up, down = shift(up, "z", 1), shift(down, "z", -1)
            below.append(up)
            above.append(down)
        last = [shift(up[:half], "z", 1), shift(down[half:], "z", -1)]
        return jnp.concatenate([down_t] + above + last + below[::-1])
    below_1, above_1 = shift(down_t, "z", 1), shift(down_t, "z", -1)
    below_2 = shift(jnp.concatenate([down_t, below_1]), "z", 2)
    above_2 = shift(jnp.concatenate([down_t, above_1]), "z", -2)
    below_4, above_4 = shift(below_2, "z", 2), shift(above_2, "z", -2)
    below_6, above_6 = shift(below_4, "z", 2), shift(above_4, "z", -2)
    far = [shift(below_4[n : n + half], "z", 3), shift(above_4[n + half :], "z", -3)]
    above = [down_t, above_1, above_2, above_4, above_6]
    below = []
    for pair in (below_6, below_4, below_2):
        below += [pair[n:], pair[:n]]
    return jnp.concatenate(above + far + below + [below_1])


def gather_by_exchange(value, axes):
    n = lax.axis_size(axes)
    spread = jnp.broadcast_to(value[None], (n,) + value.shape)
    return lax.all_to_all(spread, axes, 0, 0, tiled=True)


def sum_by_exchange(value, axes):
    n = lax.axis_size(axes)
    parts = value.astype(bf16).reshape(n, value.shape[0] // n, value.shape[1])
    return jnp.sum(lax.all_to_all(parts, axes, 0, 0, tiled=True).astype(f32), axis=0)


def on_device(activations, down_proj, precond, target):
    tokens, features = activations.shape
    rank = precond.shape[0]
    nf, nz = lax.axis_size(FEAT), lax.axis_size("z")
    feat = lax.axis_index(FEAT)
    core = lax.axis_index("core")
    share = rank // nf
    narrow = down_proj.shape[1]

    partner = swap(activations, "yhi")
    mine = gather_columns(down_proj.T)
    columns_t = jnp.concatenate([mine, swap(mine, "core")])
    partial_map = jnp.stack(
        [
            dot(part, columns_t, 1, 1).astype(bf16).reshape(nf, tokens // nf, rank // 2)
            for part in (activations, partner)
        ],
        axis=1,
    )
    share_rel = sum_by_exchange(partial_map.reshape(2 * tokens, rank // 2), FEAT).astype(bf16)

    quarter = rank // 4
    start = quarter - lax.axis_index("z") * narrow
    turned = [
        lax.dynamic_slice_in_dim(jnp.concatenate([part, part], axis=1), start, quarter, 1)
        for part in (share_rel[:, :quarter], share_rel[:, quarter:])
    ]
    turned = jnp.concatenate(ordered(core == 0, *turned), axis=1)
    own, other = turned[: tokens // nf], turned[tokens // nf :]
    spread = jnp.stack(ordered(lax.axis_index("yhi") == 0, own, other))
    spread = jnp.broadcast_to(spread[None], (nf,) + spread.shape)
    plane = ("x", "ylo", "yhi")
    halves = lax.all_to_all(
        spread.reshape(2 * nf, tokens // nf, rank // 2), plane, 0, 0, tiled=True
    ).reshape(nf, 2, tokens // nf, rank // 2)
    joined = jnp.concatenate([halves[:, 0], halves[:, 1]], axis=2).reshape(tokens, rank)

    rows = precond.reshape(2, nz, 2, narrow, rank).transpose(0, 2, 1, 3, 4).reshape(rank, rank)

    joined_slice = lax.dynamic_slice_in_dim(joined, feat * share, share, 1)
    total = dot(joined_slice, jnp.concatenate([joined, target], axis=1), 0, 0)
    width = total.shape[1]
    summed = sum_by_exchange(sum_by_exchange(total, ("core", "yhi")), "z").astype(bf16)
    summed = gather_by_exchange(summed, "z").reshape(share // 4, width)
    summed = gather_by_exchange(summed, plane).reshape(nf, share // 2, width)
    low, high = ordered(core == 0, summed, swap(summed, "core"))
    summed = jnp.stack([low, high], axis=1).reshape(rank, width)
    gram = summed[:, :rank]
    back = summed[:, rank:]

    descent = dot(rows, back, 0, 0)
    gram_now = dot(descent, descent, 0, 0, three)
    lift = dot(rows, descent.astype(bf16), 1, 0)
    lift_b = lift.astype(bf16)
    image_back = dot(gram, lift_b, 1, 0)
    curvature = dot(lift_b.astype(f32), image_back, 0, 0, three)
    inverse = invert(curvature)
    step = dot(inverse, gram_now, 1, 0, three)

    coarse = image_back.astype(bf16)
    fine = (image_back - coarse.astype(f32)).astype(bf16)
    curved = dot(rows, coarse, 0, 0) + dot(rows, fine, 0, 0)
    descent_next = descent - dot(curved, step, 1, 0, three)
    gram_next = dot(descent_next, descent_next, 0, 0, three)
    mixing = dot(inverse, dot(curved, descent_next, 0, 0, three), 1, 0, three)
    direction = descent_next - dot(descent, mixing, 1, 0, three)
    lift_next = dot(rows, direction.astype(bf16), 1, 0)
    lift_b = lift_next.astype(bf16)
    curvature = dot(lift_b.astype(f32), dot(gram, lift_b, 1, 0), 0, 0, three)
    step_next = dot(invert(curvature), gram_next, 1, 0, three)

    coefficients = dot(lift, step, 1, 0, three) + dot(lift_next, step_next, 1, 0, three)
    residual = target.astype(f32) - dot(joined, coefficients.astype(bf16), 1, 0)
    part = nz * 2 // nf
    kept = coefficients.reshape(2, 2, nz, narrow, -1).transpose(0, 2, 1, 3, 4)
    kept = kept.reshape(nf, part, 2, narrow, -1)
    solution = lax.dynamic_index_in_dim(kept, feat, 0, keepdims=False).reshape(share, -1)
    return solution, residual


def solution(mesh):
    ntok, nfeat = mesh.devices.shape
    fine = Mesh(mesh.devices.reshape(2, ntok // 4, 2, nfeat // 2, 2), AXES)
    return jax.shard_map(
        on_device,
        mesh=fine,
        in_specs=(P(TOK, FEAT), P(FEAT, TOK), P(), P(TOK, None)),
        out_specs=(P(FEAT, None), P(TOK, None)),
        check_vma=False,
    )
```

```python
import jax
import jax.numpy as jnp
from jax import lax
from jax.experimental import pallas as pl
from jax.experimental.pallas import tpu as pltpu
from jax.sharding import Mesh, PartitionSpec as P

AXES = ("yhi", "z", "core", "x", "ylo")
TOK = ("yhi", "z", "core")
FEAT = ("x", "ylo")
bf16 = jnp.bfloat16
f32 = jnp.float32
precise = lax.Precision.HIGHEST
three = lax.Precision.HIGH


def dot(a, b, ca, cb, precision=None):
    return lax.dot_general(
        a, b, (((ca,), (cb,)), ((), ())), precision=precision, preferred_element_type=f32
    )


def invert_block(d):
    n = d.shape[0]
    lanes = lax.broadcasted_iota(jnp.int32, (8, n), 1)
    subs = lax.broadcasted_iota(jnp.int32, (8, n), 0)

    def lane(v, j):
        return jnp.broadcast_to(v[:, j : j + 1], (8, n))

    def row(v, j):
        return jnp.broadcast_to(v[j : j + 1, :], (8, n))

    tiles = [d[i : i + 8, :] for i in range(0, n, 8)]
    count = len(tiles)
    for p in range(count):
        lo = 8 * p
        pivots = [lane(tiles[p], lo + k) for k in range(8)]
        for j in range(8):
            at = subs == j
            scale = 1.0 / row(pivots[j], j)
            minus = -pivots[j]
            fresh = []
            for k in range(8):
                if k == j:
                    fresh.append(jnp.where(at, scale, minus * scale))
                else:
                    scaled = row(pivots[k], j) * scale
                    fresh.append(jnp.where(at, scaled, pivots[k] + minus * scaled))
            pivots = fresh
        inside = (lanes >= lo) & (lanes < lo + 8)
        panel = jnp.where(inside, jnp.where(lanes - lo == subs, 1.0, 0.0), tiles[p])
        scaled = pivots[0] * row(panel, 0)
        for k in range(1, 8):
            scaled = scaled + pivots[k] * row(panel, k)
        rows = [row(scaled, k) for k in range(8)]
        for i in [(p + 1 + i) % count for i in range(count - 1)]:
            even = lane(tiles[i], lo) * rows[0]
            odd = lane(tiles[i], lo + 1) * rows[1]
            for k in range(2, 8, 2):
                even = even + lane(tiles[i], lo + k) * rows[k]
                odd = odd + lane(tiles[i], lo + k + 1) * rows[k + 1]
            tiles[i] = jnp.where(inside, 0.0, tiles[i]) - (even + odd)
        tiles[p] = scaled
    return jnp.concatenate(tiles, axis=0)


def invert_kernel(matrix_ref, out_ref):
    half = matrix_ref.shape[0] // 2
    first = invert_block(matrix_ref[:half, :half])
    corner = matrix_ref[:half, half:]
    right = dot(first, corner, 1, 0, precise)
    last = invert_block(matrix_ref[half:, half:] - dot(corner, right, 0, 0, precise))
    cross = dot(right, last, 1, 0, precise)
    out_ref[:half, :half] = first + dot(cross, right, 1, 1, precise)
    out_ref[:half, half:] = -cross
    out_ref[half:, :half] = -cross.T
    out_ref[half:, half:] = last


def invert(matrix):
    return pl.pallas_call(
        invert_kernel,
        out_shape=jax.ShapeDtypeStruct(matrix.shape, f32),
        in_specs=[pl.BlockSpec(memory_space=pltpu.VMEM)],
        out_specs=pl.BlockSpec(memory_space=pltpu.VMEM),
        compiler_params=pltpu.CompilerParams(vmem_limit_bytes=16 * 1024 * 1024),
    )(matrix)


def swap(value, axis):
    return lax.ppermute(value, axis, [(0, 1), (1, 0)])


def ordered(first, mine, other):
    return jnp.where(first, mine, other), jnp.where(first, other, mine)


def shift(value, axis, by):
    n = lax.axis_size(axis)
    return lax.ppermute(value, axis, [(i, (i + by) % n) for i in range(n)])


def gather_columns(down_t):
    n = down_t.shape[0]
    half = n // 2
    nz = lax.axis_size("z")
    if nz != 16:
        up, down = down_t, down_t
        below, above = [], []
        for k in range(1, nz // 2):
            up, down = shift(up, "z", 1), shift(down, "z", -1)
            below.append(up)
            above.append(down)
        last = [shift(up[:half], "z", 1), shift(down[half:], "z", -1)]
        return jnp.concatenate([down_t] + above + last + below[::-1])
    below_1, above_1 = shift(down_t, "z", 1), shift(down_t, "z", -1)
    below_2 = shift(jnp.concatenate([down_t, below_1]), "z", 2)
    above_2 = shift(jnp.concatenate([down_t, above_1]), "z", -2)
    below_4, above_4 = shift(below_2, "z", 2), shift(above_2, "z", -2)
    below_6, above_6 = shift(below_4, "z", 2), shift(above_4, "z", -2)
    far = [shift(below_6[n : n + half], "z", 1), shift(above_6[n + half :], "z", -1)]
    above = [down_t, above_1, above_2, above_4, above_6]
    below = []
    for pair in (below_6, below_4, below_2):
        below += [pair[n:], pair[:n]]
    return jnp.concatenate(above + far + below + [below_1])


def gather_by_exchange(value, axes):
    n = lax.axis_size(axes)
    spread = jnp.broadcast_to(value[None], (n,) + value.shape)
    return lax.all_to_all(spread, axes, 0, 0, tiled=True)


def sum_by_exchange(value, axes):
    n = lax.axis_size(axes)
    parts = value.astype(bf16).reshape(n, value.shape[0] // n, value.shape[1])
    return jnp.sum(lax.all_to_all(parts, axes, 0, 0, tiled=True).astype(f32), axis=0)


def on_device(activations, down_proj, precond, target):
    tokens, features = activations.shape
    rank = precond.shape[0]
    nf, nz = lax.axis_size(FEAT), lax.axis_size("z")
    feat = lax.axis_index(FEAT)
    core = lax.axis_index("core")
    share = rank // nf
    narrow = down_proj.shape[1]

    partner = swap(activations, "yhi")
    mine = gather_columns(down_proj.T)
    columns_t = jnp.concatenate([mine, swap(mine, "core")])
    partial_map = jnp.stack(
        [
            dot(part, columns_t, 1, 1).astype(bf16).reshape(nf, tokens // nf, rank // 2)
            for part in (activations, partner)
        ],
        axis=1,
    )
    share_rel = sum_by_exchange(partial_map.reshape(2 * tokens, rank // 2), FEAT).astype(bf16)

    quarter = rank // 4
    start = quarter - lax.axis_index("z") * narrow
    turned = [
        lax.dynamic_slice_in_dim(jnp.concatenate([part, part], axis=1), start, quarter, 1)
        for part in (share_rel[:, :quarter], share_rel[:, quarter:])
    ]
    turned = jnp.concatenate(ordered(core == 0, *turned), axis=1)
    own, other = turned[: tokens // nf], turned[tokens // nf :]
    spread = jnp.stack(ordered(lax.axis_index("yhi") == 0, own, other))
    spread = jnp.broadcast_to(spread[None], (nf,) + spread.shape)
    plane = ("x", "ylo", "yhi")
    halves = lax.all_to_all(
        spread.reshape(2 * nf, tokens // nf, rank // 2), plane, 0, 0, tiled=True
    ).reshape(nf, 2, tokens // nf, rank // 2)
    joined = jnp.concatenate([halves[:, 0], halves[:, 1]], axis=2).reshape(tokens, rank)

    rows = precond.reshape(2, nz, 2, narrow, rank).transpose(0, 2, 1, 3, 4).reshape(rank, rank)

    joined_slice = lax.dynamic_slice_in_dim(joined, feat * share, share, 1)
    total = dot(joined_slice, jnp.concatenate([joined, target], axis=1), 0, 0)
    width = total.shape[1]
    summed = sum_by_exchange(sum_by_exchange(total, ("core", "yhi")), "z").astype(bf16)
    summed = gather_by_exchange(summed, "z").reshape(share // 4, width)
    summed = gather_by_exchange(summed, plane).reshape(nf, share // 2, width)
    low, high = ordered(core == 0, summed, swap(summed, "core"))
    summed = jnp.stack([low, high], axis=1).reshape(rank, width)
    gram = summed[:, :rank]
    back = summed[:, rank:]

    descent = dot(rows, back, 0, 0)
    gram_now = dot(descent, descent, 0, 0, three)
    lift = dot(rows, descent.astype(bf16), 1, 0)
    lift_b = lift.astype(bf16)
    image_back = dot(gram, lift_b, 1, 0)
    curvature = dot(lift_b.astype(f32), image_back, 0, 0, three)
    inverse = invert(curvature)
    step = dot(inverse, gram_now, 1, 0, three)

    curved = dot(rows, image_back.astype(bf16), 0, 0)
    descent_next = descent - dot(curved, step, 1, 0, three)
    gram_next = dot(descent_next, descent_next, 0, 0, three)
    mixing = dot(inverse, dot(curved, descent_next, 0, 0, three), 1, 0, three)
    direction = descent_next - dot(descent, mixing, 1, 0, three)
    lift_next = dot(rows, direction.astype(bf16), 1, 0)
    lift_b = lift_next.astype(bf16)
    curvature = dot(lift_b.astype(f32), dot(gram, lift_b, 1, 0), 0, 0, three)
    step_next = dot(invert(curvature), gram_next, 1, 0, three)

    coefficients = dot(lift, step, 1, 0, three) + dot(lift_next, step_next, 1, 0, three)
    residual = target.astype(f32) - dot(joined, coefficients.astype(bf16), 1, 0)
    part = nz * 2 // nf
    kept = coefficients.reshape(2, 2, nz, narrow, -1).transpose(0, 2, 1, 3, 4)
    kept = kept.reshape(nf, part, 2, narrow, -1)
    solution = lax.dynamic_index_in_dim(kept, feat, 0, keepdims=False).reshape(share, -1)
    return solution, residual


def solution(mesh):
    ntok, nfeat = mesh.devices.shape
    fine = Mesh(mesh.devices.reshape(2, ntok // 4, 2, nfeat // 2, 2), AXES)
    return jax.shard_map(
        on_device,
        mesh=fine,
        in_specs=(P(TOK, FEAT), P(FEAT, TOK), P(), P(TOK, None)),
        out_specs=(P(FEAT, None), P(TOK, None)),
        check_vma=False,
    )
```

```python
import jax
import jax.numpy as jnp
from jax import lax
from jax.experimental import pallas as pl
from jax.experimental.pallas import tpu as pltpu
from jax.sharding import Mesh, PartitionSpec as P

AXES = ("yhi", "z", "core", "x", "ylo")
TOK = ("yhi", "z", "core")
FEAT = ("x", "ylo")
bf16 = jnp.bfloat16
f32 = jnp.float32
precise = lax.Precision.HIGHEST
three = lax.Precision.HIGH


def dot(a, b, ca, cb, precision=None):
    return lax.dot_general(
        a, b, (((ca,), (cb,)), ((), ())), precision=precision, preferred_element_type=f32
    )


def invert_block(d):
    n = d.shape[0]
    lanes = lax.broadcasted_iota(jnp.int32, (8, n), 1)
    subs = lax.broadcasted_iota(jnp.int32, (8, n), 0)

    def lane(v, j):
        return jnp.broadcast_to(v[:, j : j + 1], (8, n))

    def row(v, j):
        return jnp.broadcast_to(v[j : j + 1, :], (8, n))

    tiles = [d[i : i + 8, :] for i in range(0, n, 8)]
    count = len(tiles)
    for p in range(count):
        lo = 8 * p
        pivots = [lane(tiles[p], lo + k) for k in range(8)]
        for j in range(8):
            at = subs == j
            scale = 1.0 / row(pivots[j], j)
            minus = -pivots[j]
            fresh = []
            for k in range(8):
                if k == j:
                    fresh.append(jnp.where(at, scale, minus * scale))
                else:
                    scaled = row(pivots[k], j) * scale
                    fresh.append(jnp.where(at, scaled, pivots[k] + minus * scaled))
            pivots = fresh
        inside = (lanes >= lo) & (lanes < lo + 8)
        panel = jnp.where(inside, jnp.where(lanes - lo == subs, 1.0, 0.0), tiles[p])
        scaled = pivots[0] * row(panel, 0)
        for k in range(1, 8):
            scaled = scaled + pivots[k] * row(panel, k)
        rows = [row(scaled, k) for k in range(8)]
        for i in [(p + 1 + i) % count for i in range(count - 1)]:
            even = lane(tiles[i], lo) * rows[0]
            odd = lane(tiles[i], lo + 1) * rows[1]
            for k in range(2, 8, 2):
                even = even + lane(tiles[i], lo + k) * rows[k]
                odd = odd + lane(tiles[i], lo + k + 1) * rows[k + 1]
            tiles[i] = jnp.where(inside, 0.0, tiles[i]) - (even + odd)
        tiles[p] = scaled
    return jnp.concatenate(tiles, axis=0)


def invert_kernel(matrix_ref, out_ref):
    half = matrix_ref.shape[0] // 2
    first = invert_block(matrix_ref[:half, :half])
    corner = matrix_ref[:half, half:]
    right = dot(first, corner, 1, 0, precise)
    last = invert_block(matrix_ref[half:, half:] - dot(corner, right, 0, 0, precise))
    cross = dot(right, last, 1, 0, precise)
    out_ref[:half, :half] = first + dot(cross, right, 1, 1, precise)
    out_ref[:half, half:] = -cross
    out_ref[half:, :half] = -cross.T
    out_ref[half:, half:] = last


def invert(matrix):
    return pl.pallas_call(
        invert_kernel,
        out_shape=jax.ShapeDtypeStruct(matrix.shape, f32),
        in_specs=[pl.BlockSpec(memory_space=pltpu.VMEM)],
        out_specs=pl.BlockSpec(memory_space=pltpu.VMEM),
        compiler_params=pltpu.CompilerParams(vmem_limit_bytes=16 * 1024 * 1024),
    )(matrix)


def join_blocks_kernel(low_ref, high_ref, gram_ref):
    count, half, _ = low_ref.shape
    size = 2 * half
    for i in range(count):
        top = i * size
        for k in range(count // 2 + 1):
            left = (i + k) % count * size
            low = low_ref[i, :, k * size : (k + 1) * size]
            high = high_ref[i, :, k * size : (k + 1) * size]
            gram_ref[top : top + half, left : left + size] = low
            gram_ref[top + half : top + size, left : left + size] = high
            if 0 < k < count // 2:
                block = jnp.concatenate([low.astype(f32), high.astype(f32)])
                gram_ref[left : left + size, top : top + size] = block.T.astype(bf16)


def join_blocks(low, high):
    rank = 2 * low.shape[0] * low.shape[1]
    return pl.pallas_call(
        join_blocks_kernel,
        out_shape=jax.ShapeDtypeStruct((rank, rank), bf16),
        in_specs=[pl.BlockSpec(memory_space=pltpu.VMEM)] * 2,
        out_specs=pl.BlockSpec(memory_space=pltpu.VMEM),
        compiler_params=pltpu.CompilerParams(vmem_limit_bytes=16 * 1024 * 1024),
    )(low, high)


def swap(value, axis):
    return lax.ppermute(value, axis, [(0, 1), (1, 0)])


def ordered(first, mine, other):
    return jnp.where(first, mine, other), jnp.where(first, other, mine)


def shift(value, axis, by):
    n = lax.axis_size(axis)
    return lax.ppermute(value, axis, [(i, (i + by) % n) for i in range(n)])


def gather_columns(down_t):
    n = down_t.shape[0]
    half = n // 2
    nz = lax.axis_size("z")
    if nz != 16:
        up, down = down_t, down_t
        below, above = [], []
        for k in range(1, nz // 2):
            up, down = shift(up, "z", 1), shift(down, "z", -1)
            below.append(up)
            above.append(down)
        last = [shift(up[:half], "z", 1), shift(down[half:], "z", -1)]
        return jnp.concatenate([down_t] + above + last + below[::-1])
    below_1, above_1 = shift(down_t, "z", 1), shift(down_t, "z", -1)
    below_2 = shift(jnp.concatenate([down_t, below_1]), "z", 2)
    above_2 = shift(jnp.concatenate([down_t, above_1]), "z", -2)
    below_4, above_4 = shift(below_2, "z", 2), shift(above_2, "z", -2)
    below_6 = shift(jnp.concatenate([below_2[n:], below_4[: n + half]]), "z", 3)
    above_6 = shift(
        jnp.concatenate([above_2[n:], above_4[:n], above_4[n + half :]]), "z", -3
    )
    above = [down_t, above_1, above_2, above_4, above_6[: 2 * n]]
    far = [below_6[2 * n :], above_6[2 * n :]]
    below = []
    for pair in (below_6, below_4, below_2):
        below += [pair[n : 2 * n], pair[:n]]
    return jnp.concatenate(above + far + below + [below_1])


def gather_by_exchange(value, axes):
    n = lax.axis_size(axes)
    spread = jnp.broadcast_to(value[None], (n,) + value.shape)
    return lax.all_to_all(spread, axes, 0, 0, tiled=True)


def sum_by_exchange(value, axes):
    n = lax.axis_size(axes)
    parts = value.astype(bf16).reshape(n, value.shape[0] // n, value.shape[1])
    return jnp.sum(lax.all_to_all(parts, axes, 0, 0, tiled=True).astype(f32), axis=0)


def on_device(activations, down_proj, precond, target):
    tokens, features = activations.shape
    rank = precond.shape[0]
    nf, nz = lax.axis_size(FEAT), lax.axis_size("z")
    feat = lax.axis_index(FEAT)
    core = lax.axis_index("core")
    share = rank // nf
    narrow = down_proj.shape[1]

    partner = swap(activations, "yhi")
    mine = gather_columns(down_proj.T)
    columns_t = jnp.concatenate([mine, swap(mine, "core")])
    partial_map = jnp.stack(
        [
            dot(part, columns_t, 1, 1).astype(bf16).reshape(nf, tokens // nf, rank // 2)
            for part in (activations, partner)
        ],
        axis=1,
    )
    share_rel = sum_by_exchange(partial_map.reshape(2 * tokens, rank // 2), FEAT).astype(bf16)

    quarter = rank // 4
    start = quarter - lax.axis_index("z") * narrow
    turned = [
        lax.dynamic_slice_in_dim(jnp.concatenate([part, part], axis=1), start, quarter, 1)
        for part in (share_rel[:, :quarter], share_rel[:, quarter:])
    ]
    turned = jnp.concatenate(ordered(core == 0, *turned), axis=1)
    own, other = turned[: tokens // nf], turned[tokens // nf :]
    spread = jnp.stack(ordered(lax.axis_index("yhi") == 0, own, other))
    spread = jnp.broadcast_to(spread[None], (nf,) + spread.shape)
    plane = ("x", "ylo", "yhi")
    halves = lax.all_to_all(
        spread.reshape(2 * nf, tokens // nf, rank // 2), plane, 0, 0, tiled=True
    ).reshape(nf, 2, tokens // nf, rank // 2)
    joined = jnp.concatenate([halves[:, 0], halves[:, 1]], axis=2).reshape(tokens, rank)

    rows = precond.reshape(2, nz, 2, narrow, rank).transpose(0, 2, 1, 3, 4).reshape(rank, rank)

    count = (nf // 2 + 1) * share
    wrapped = jnp.concatenate([joined, joined[:, : count - share]], axis=1)
    window = lax.dynamic_slice_in_dim(wrapped, feat * share, count, 1)
    total = dot(window[:, :share], jnp.concatenate([window, target], axis=1), 0, 0)
    width = total.shape[1]
    summed = sum_by_exchange(sum_by_exchange(total, ("core", "yhi")), "z").astype(bf16)
    summed = gather_by_exchange(summed, "z").reshape(share // 4, width)
    summed = gather_by_exchange(summed, plane).reshape(nf, share // 2, width)
    low, high = ordered(core == 0, summed, swap(summed, "core"))
    gram = join_blocks(low, high)
    back = jnp.stack([low[:, :, count:], high[:, :, count:]], axis=1).reshape(rank, -1)

    descent = dot(rows, back, 0, 0)
    gram_now = dot(descent, descent, 0, 0, three)
    lift = dot(rows, descent.astype(bf16), 1, 0)
    lift_b = lift.astype(bf16)
    image_back = dot(gram, lift_b, 1, 0)
    curvature = dot(lift_b.astype(f32), image_back, 0, 0, three)
    inverse = invert(curvature)
    step = dot(inverse, gram_now, 1, 0, three)

    curved = dot(rows, image_back.astype(bf16), 0, 0)
    descent_next = descent - dot(curved, step, 1, 0, three)
    gram_next = dot(descent_next, descent_next, 0, 0, three)
    mixing = dot(inverse, dot(curved, descent_next, 0, 0, three), 1, 0, three)
    direction = descent_next - dot(descent, mixing, 1, 0, three)
    lift_next = dot(rows, direction.astype(bf16), 1, 0)
    lift_b = lift_next.astype(bf16)
    curvature = dot(lift_b.astype(f32), dot(gram, lift_b, 1, 0), 0, 0, three)
    step_next = dot(invert(curvature), gram_next, 1, 0, three)

    coefficients = dot(lift, step, 1, 0, three) + dot(lift_next, step_next, 1, 0, three)
    residual = target.astype(f32) - dot(joined, coefficients.astype(bf16), 1, 0)
    part = nz * 2 // nf
    kept = coefficients.reshape(2, 2, nz, narrow, -1).transpose(0, 2, 1, 3, 4)
    kept = kept.reshape(nf, part, 2, narrow, -1)
    solution = lax.dynamic_index_in_dim(kept, feat, 0, keepdims=False).reshape(share, -1)
    return solution, residual


def solution(mesh):
    ntok, nfeat = mesh.devices.shape
    fine = Mesh(mesh.devices.reshape(2, ntok // 4, 2, nfeat // 2, 2), AXES)
    return jax.shard_map(
        on_device,
        mesh=fine,
        in_specs=(P(TOK, FEAT), P(FEAT, TOK), P(), P(TOK, None)),
        out_specs=(P(FEAT, None), P(TOK, None)),
        check_vma=False,
    )
```

```python
import jax
import jax.numpy as jnp
from jax import lax
from jax.experimental import pallas as pl
from jax.experimental.pallas import tpu as pltpu
from jax.sharding import Mesh, PartitionSpec as P

AXES = ("yhi", "z", "core", "x", "ylo")
TOK = ("yhi", "z", "core")
FEAT = ("x", "ylo")
bf16 = jnp.bfloat16
f32 = jnp.float32
precise = lax.Precision.HIGHEST
three = lax.Precision.HIGH


def dot(a, b, ca, cb, precision=None):
    return lax.dot_general(
        a, b, (((ca,), (cb,)), ((), ())), precision=precision, preferred_element_type=f32
    )


def invert_block(d):
    n = d.shape[0]
    lanes = lax.broadcasted_iota(jnp.int32, (8, n), 1)
    subs = lax.broadcasted_iota(jnp.int32, (8, n), 0)

    def lane(v, j):
        return jnp.broadcast_to(v[:, j : j + 1], (8, n))

    def row(v, j):
        return jnp.broadcast_to(v[j : j + 1, :], (8, n))

    tiles = [d[i : i + 8, :] for i in range(0, n, 8)]
    count = len(tiles)
    for p in range(count):
        lo = 8 * p
        pivots = [lane(tiles[p], lo + k) for k in range(8)]
        for j in range(8):
            at = subs == j
            scale = 1.0 / row(pivots[j], j)
            minus = -pivots[j]
            fresh = []
            for k in range(8):
                if k == j:
                    fresh.append(jnp.where(at, scale, minus * scale))
                else:
                    scaled = row(pivots[k], j) * scale
                    fresh.append(jnp.where(at, scaled, pivots[k] + minus * scaled))
            pivots = fresh
        inside = (lanes >= lo) & (lanes < lo + 8)
        panel = jnp.where(inside, jnp.where(lanes - lo == subs, 1.0, 0.0), tiles[p])
        scaled = pivots[0] * row(panel, 0)
        for k in range(1, 8):
            scaled = scaled + pivots[k] * row(panel, k)
        rows = [row(scaled, k) for k in range(8)]
        for i in [(p + 1 + i) % count for i in range(count - 1)]:
            even = lane(tiles[i], lo) * rows[0]
            odd = lane(tiles[i], lo + 1) * rows[1]
            for k in range(2, 8, 2):
                even = even + lane(tiles[i], lo + k) * rows[k]
                odd = odd + lane(tiles[i], lo + k + 1) * rows[k + 1]
            tiles[i] = jnp.where(inside, 0.0, tiles[i]) - (even + odd)
        tiles[p] = scaled
    return jnp.concatenate(tiles, axis=0)


def invert_kernel(matrix_ref, out_ref):
    half = matrix_ref.shape[0] // 2
    first = invert_block(matrix_ref[:half, :half])
    corner = matrix_ref[:half, half:]
    right = dot(first, corner, 1, 0, precise)
    last = invert_block(matrix_ref[half:, half:] - dot(corner, right, 0, 0, precise))
    cross = dot(right, last, 1, 0, precise)
    out_ref[:half, :half] = first + dot(cross, right, 1, 1, precise)
    out_ref[:half, half:] = -cross
    out_ref[half:, :half] = -cross.T
    out_ref[half:, half:] = last


def invert(matrix):
    return pl.pallas_call(
        invert_kernel,
        out_shape=jax.ShapeDtypeStruct(matrix.shape, f32),
        in_specs=[pl.BlockSpec(memory_space=pltpu.VMEM)],
        out_specs=pl.BlockSpec(memory_space=pltpu.VMEM),
        compiler_params=pltpu.CompilerParams(vmem_limit_bytes=16 * 1024 * 1024),
    )(matrix)


def join_blocks_kernel(core_ref, mine_ref, other_ref, gram_ref, back_ref):
    count, half, _ = mine_ref.shape
    size = 2 * half
    width = (count // 2 + 1) * size

    def join(low_ref, high_ref):
        for i in range(count):
            top = i * size
            back_ref[top : top + half, :] = low_ref[i, :, width:]
            back_ref[top + half : top + size, :] = high_ref[i, :, width:]
            for k in range(count // 2 + 1):
                left = (i + k) % count * size
                low = low_ref[i, :, k * size : (k + 1) * size]
                high = high_ref[i, :, k * size : (k + 1) * size]
                gram_ref[top : top + half, left : left + size] = low
                gram_ref[top + half : top + size, left : left + size] = high
                if 0 < k < count // 2:
                    block = jnp.concatenate([low.astype(f32), high.astype(f32)])
                    gram_ref[left : left + size, top : top + size] = block.T.astype(bf16)

    @pl.when(core_ref[0] == 0)
    def _():
        join(mine_ref, other_ref)

    @pl.when(core_ref[0] != 0)
    def _():
        join(other_ref, mine_ref)


def join_blocks(core, mine, other, columns):
    rank = 2 * mine.shape[0] * mine.shape[1]
    vmem = pl.BlockSpec(memory_space=pltpu.VMEM)
    return pl.pallas_call(
        join_blocks_kernel,
        out_shape=[
            jax.ShapeDtypeStruct((rank, rank), bf16),
            jax.ShapeDtypeStruct((rank, columns), bf16),
        ],
        in_specs=[pl.BlockSpec(memory_space=pltpu.SMEM), vmem, vmem],
        out_specs=[vmem, vmem],
        compiler_params=pltpu.CompilerParams(vmem_limit_bytes=16 * 1024 * 1024),
    )(core.reshape(1), mine, other)


def swap(value, axis):
    return lax.ppermute(value, axis, [(0, 1), (1, 0)])


def ordered(first, mine, other):
    return jnp.where(first, mine, other), jnp.where(first, other, mine)


def shift(value, axis, by):
    n = lax.axis_size(axis)
    return lax.ppermute(value, axis, [(i, (i + by) % n) for i in range(n)])


def gather_columns(down_t):
    n = down_t.shape[0]
    half = n // 2
    nz = lax.axis_size("z")
    if nz != 16:
        up, down = down_t, down_t
        below, above = [], []
        for k in range(1, nz // 2):
            up, down = shift(up, "z", 1), shift(down, "z", -1)
            below.append(up)
            above.append(down)
        last = [shift(up[:half], "z", 1), shift(down[half:], "z", -1)]
        return jnp.concatenate([down_t] + above + last + below[::-1])
    below_1, above_1 = shift(down_t, "z", 1), shift(down_t, "z", -1)
    below_2 = shift(jnp.concatenate([down_t, below_1]), "z", 2)
    above_2 = shift(jnp.concatenate([down_t, above_1]), "z", -2)
    below_4, above_4 = shift(below_2, "z", 2), shift(above_2, "z", -2)
    below_6 = shift(jnp.concatenate([below_2[n:], below_4[: n + half]]), "z", 3)
    above_6 = shift(
        jnp.concatenate([above_2[n:], above_4[:n], above_4[n + half :]]), "z", -3
    )
    above = [down_t, above_1, above_2, above_4, above_6[: 2 * n]]
    far = [below_6[2 * n :], above_6[2 * n :]]
    below = []
    for pair in (below_6, below_4, below_2):
        below += [pair[n : 2 * n], pair[:n]]
    return jnp.concatenate(above + far + below + [below_1])


def gather_by_exchange(value, axes):
    n = lax.axis_size(axes)
    spread = jnp.broadcast_to(value[None], (n,) + value.shape)
    return lax.all_to_all(spread, axes, 0, 0, tiled=True)


def sum_by_exchange(value, axes):
    n = lax.axis_size(axes)
    parts = value.astype(bf16).reshape(n, value.shape[0] // n, value.shape[1])
    return jnp.sum(lax.all_to_all(parts, axes, 0, 0, tiled=True).astype(f32), axis=0)


def on_device(activations, down_proj, precond, target):
    tokens, features = activations.shape
    rank = precond.shape[0]
    nf, nz = lax.axis_size(FEAT), lax.axis_size("z")
    feat = lax.axis_index(FEAT)
    core = lax.axis_index("core")
    share = rank // nf
    narrow = down_proj.shape[1]

    partner = swap(activations, "yhi")
    mine = gather_columns(down_proj.T)
    columns_t = jnp.concatenate([mine, swap(mine, "core")])
    partial_map = jnp.stack(
        [
            dot(part, columns_t, 1, 1).astype(bf16).reshape(nf, tokens // nf, rank // 2)
            for part in (activations, partner)
        ],
        axis=1,
    )
    share_rel = sum_by_exchange(partial_map.reshape(2 * tokens, rank // 2), FEAT).astype(bf16)

    quarter = rank // 4
    start = quarter - lax.axis_index("z") * narrow
    turned = [
        lax.dynamic_slice_in_dim(jnp.concatenate([part, part], axis=1), start, quarter, 1)
        for part in (share_rel[:, :quarter], share_rel[:, quarter:])
    ]
    turned = jnp.concatenate(ordered(core == 0, *turned), axis=1)
    own, other = turned[: tokens // nf], turned[tokens // nf :]
    spread = jnp.stack(ordered(lax.axis_index("yhi") == 0, own, other))
    spread = jnp.broadcast_to(spread[None], (nf,) + spread.shape)
    plane = ("x", "ylo", "yhi")
    halves = lax.all_to_all(
        spread.reshape(2 * nf, tokens // nf, rank // 2), plane, 0, 0, tiled=True
    ).reshape(nf, 2, tokens // nf, rank // 2)
    joined = jnp.concatenate([halves[:, 0], halves[:, 1]], axis=2).reshape(tokens, rank)

    rows = precond.reshape(2, nz, 2, narrow, rank).transpose(0, 2, 1, 3, 4).reshape(rank, rank)

    count = (nf // 2 + 1) * share
    wrapped = jnp.concatenate([joined, joined[:, : count - share]], axis=1)
    window = lax.dynamic_slice_in_dim(wrapped, feat * share, count, 1)
    total = dot(window[:, :share], jnp.concatenate([window, target], axis=1), 0, 0)
    width = total.shape[1]
    summed = sum_by_exchange(sum_by_exchange(total, ("core", "yhi")), "z").astype(bf16)
    summed = gather_by_exchange(summed, "z").reshape(share // 4, width)
    summed = gather_by_exchange(summed, plane).reshape(nf, share // 2, width)
    gram, back = join_blocks(core, summed, swap(summed, "core"), target.shape[1])

    descent = dot(rows, back, 0, 0)
    gram_now = dot(descent, descent, 0, 0, three)
    lift = dot(rows, descent.astype(bf16), 1, 0)
    lift_b = lift.astype(bf16)
    image_back = dot(gram, lift_b, 1, 0)
    curvature = dot(lift_b.astype(f32), image_back, 0, 0, three)
    inverse = invert(curvature)
    step = dot(inverse, gram_now, 1, 0, three)

    curved = dot(rows, image_back.astype(bf16), 0, 0)
    descent_next = descent - dot(curved, step, 1, 0, three)
    gram_next = dot(descent_next, descent_next, 0, 0, three)
    mixing = dot(inverse, dot(curved, descent_next, 0, 0, three), 1, 0, three)
    direction = descent_next - dot(descent, mixing, 1, 0, three)
    lift_next = dot(rows, direction.astype(bf16), 1, 0)
    lift_b = lift_next.astype(bf16)
    curvature = dot(lift_b.astype(f32), dot(gram, lift_b, 1, 0), 0, 0, three)
    step_next = dot(invert(curvature), gram_next, 1, 0, three)

    coefficients = dot(lift, step, 1, 0, three) + dot(lift_next, step_next, 1, 0, three)
    residual = target.astype(f32) - dot(joined, coefficients.astype(bf16), 1, 0)
    part = nz * 2 // nf
    kept = coefficients.reshape(2, 2, nz, narrow, -1).transpose(0, 2, 1, 3, 4)
    kept = kept.reshape(nf, part, 2, narrow, -1)
    solution = lax.dynamic_index_in_dim(kept, feat, 0, keepdims=False).reshape(share, -1)
    return solution, residual


def solution(mesh):
    ntok, nfeat = mesh.devices.shape
    fine = Mesh(mesh.devices.reshape(2, ntok // 4, 2, nfeat // 2, 2), AXES)
    return jax.shard_map(
        on_device,
        mesh=fine,
        in_specs=(P(TOK, FEAT), P(FEAT, TOK), P(), P(TOK, None)),
        out_specs=(P(FEAT, None), P(TOK, None)),
        check_vma=False,
    )
```
